32 devices in a mesh: occ: 16 (over z, y, x), vir: 2 (over core).
Axes of the slice: x: 2, y: 2, z: 4, core: 2. Of those that a mesh axis runs over, the one named last changes fastest.
Arguments:
- amplitudes: float32 [2304, 384, 384], P('occ', 'vir'), may hold values from -6 to 6
- integrals: float32 [384, 384, 1536], P('vir', 'occ'), may hold values from -0.015625 to 0.015625
Outputs:
- ladder: float32 [2304, 1536], P('occ', 'vir')
The draws below stay inside these ranges and needn't reach their ends.
All inputs are finite; a program needn't handle non-finite values.
Results may differ from the reference program's by a relative error of at most 0.000071.
Values sent between devices are 32-bit elements; how exact they have to be, the bound alone decides.
No kernel may reach another device: no remote copies, remote signals or barrier semaphores. Data moves between devices by JAX's collectives and lax.ppermute only.
A program may use at most 384 MiB of HBM per device.

```python
import jax
import jax.numpy as jnp
from jax import lax

O = 48
V = 384
SLAB = 4
PAIRS = 2304


def levels(stream_key, extent, pieces, least, top_value):
    factor_of, own = 1.0, jax.random.fold_in(stream_key, 6)
    for axis_at, shards_of in pieces:
        heights = jnp.exp(jax.random.uniform(jax.random.fold_in(own, axis_at), (shards_of,), jnp.float32, least / len(pieces), top_value / len(pieces)))
        factor_of = factor_of * jnp.repeat(heights, extent[axis_at] // shards_of).reshape([-1 if axis == axis_at else 1 for axis in range(len(extent))])
    return factor_of


def centred(stream_key, dims, width, bound, shards=(), held_as=jnp.bfloat16):
    result = jax.random.normal(stream_key, dims, jnp.float32) * width
    if len(shards) > 0:
        result = levels(stream_key, dims, shards, -0.22, 0.18) * result
    return jnp.clip(result, min=-bound, max=bound).astype(held_as)


def setup_inputs(seed: int = 0) -> dict:
    keys = jax.random.split(jax.random.key(seed), 3)
    return {
        "amplitudes": centred(keys[0], (PAIRS, V, V), 1.0, 6.0, ((0, 16), (1, 2)), jnp.float32),
        "integrals": centred(keys[1], (V, V, SLAB * V), (V * V) ** -0.5, 0.015625, ((0, 2), (1, 16)), jnp.float32),
    }


def reference(amplitudes, integrals):
    grouped = amplitudes.reshape(O, O, V * V)
    symmetric = (grouped + jnp.transpose(grouped, (1, 0, 2))).reshape(PAIRS, V * V)
    slab_matrix = integrals.reshape(V * V, SLAB * V)
    return jnp.dot(symmetric, slab_matrix, precision=lax.Precision.HIGHEST, preferred_element_type=jnp.float32)
```

```python
import numpy as np
import jax
import jax.numpy as jnp
from jax import lax
from jax.experimental import pallas as pl
from jax.experimental.pallas import tpu as pltpu
from jax.sharding import PartitionSpec as P

O = 48
PLANES = 4
SPOTS = 4
OWNERS = PLANES * SPOTS
SHARE = O // OWNERS
CG = 16
SUB = 8
CHUNK = 2 * CG
VMEM = 56 * 1024 * 1024

CLASSES = ((0, 0), (1, 1), (0, 1), (0, 2), (1, 2), (2, 2))
BATCH_ENDS = ((0, 1), (0, 2), (1, 2), (2, 2))


def pack_kernel(where_ref, *refs):
    z, q = where_ref[0], where_ref[1]
    a_refs, x_refs, turned = refs[:3], refs[-SPOTS - 1 : -1], refs[-1]
    rows, cs, _ = a_refs[0].shape
    lanes = 128 * len(a_refs)
    width = lanes // OWNERS
    flat = [a_ref.reshape(rows * cs, 128) for a_ref in a_refs]
    lane = lax.broadcasted_iota(jnp.int32, (SUB, lanes), 1)
    block = (lane * (65536 // width + 1)) >> 16
    low = lax.broadcasted_iota(jnp.int32, (SUB, lanes), 0) < 4

    def step(half, carry):
        for cg in range(2):
            first = half * SUB * cs + cg * CG
            t = [
                jnp.concatenate([ref[pl.ds(first + c, SUB, stride=cs), :] for ref in flat], axis=1)
                for c in range(CG)
            ]
            for bit in (8, 4, 2, 1):
                keep = (block & bit) == 0
                for c in range(CG):
                    if c & bit == 0:
                        a, b = t[c], t[c + bit]
                        t[c] = jnp.where(keep, a, pltpu.roll(b, bit * width, 1))
                        t[c + bit] = jnp.where(keep, pltpu.roll(a, lanes - bit * width, 1), b)
            for o in range(OWNERS):
                turned[cg, o] = t[o]
        for m, x_ref in enumerate(x_refs):
            for dr in range(PLANES):
                o = (z ^ dr) * SPOTS + (q ^ m)
                t0, t1 = turned[0, o], turned[1, o]
                x_ref[dr, z ^ (2 * half)] = jnp.where(low, t0, pltpu.roll(t1, 4, 0))
                x_ref[dr, z ^ (2 * half + 1)] = jnp.where(low, pltpu.roll(t0, 4, 0), t1)
        return carry

    lax.fori_loop(0, 2, step, 0)


def pack(where, amplitudes, pair, span, after):
    r, s = pair
    both = 1 if r == s else 2
    rows, cs, lanes = amplitudes.shape
    begin, deep = span[0], span[1] - span[0]
    view = amplitudes.reshape(SHARE, OWNERS, SHARE, cs, lanes)
    shape = (PLANES, PLANES, both, deep, SUB, lanes)
    block = pl.BlockSpec(
        (PLANES, PLANES, None, None, SUB, lanes), lambda u, k, w: (0, 0, u, k, 0, 0)
    )
    in_specs = [
        pl.BlockSpec(
            (None, OWNERS, None, CHUNK, 128),
            lambda u, k, w, at=at: (r + u * (s - r), 0, s + u * (r - s), begin + k, at),
        )
        for at in range(lanes // 128)
    ]
    operands = [view] * len(in_specs) + after
    in_specs += [pl.BlockSpec(memory_space=pl.ANY)] * len(after)
    return pl.pallas_call(
        pack_kernel,
        out_shape=[jax.ShapeDtypeStruct(shape, jnp.float32)] * SPOTS,
        grid_spec=pltpu.PrefetchScalarGridSpec(
            num_scalar_prefetch=1,
            grid=(both, deep),
            in_specs=in_specs,
            out_specs=[block] * SPOTS,
            scratch_shapes=[pltpu.VMEM((2, OWNERS, SUB, lanes), jnp.float32)],
        ),
        compiler_params=pltpu.CompilerParams(vmem_limit_bytes=VMEM),
        cost_estimate=pl.CostEstimate(
            flops=0, transcendentals=0, bytes_accessed=0
        ),
        name="pack",
    )(where, *operands)


def hold(arrays, after):
    def kernel(*refs):
        pass

    return pl.pallas_call(
        kernel,
        out_shape=[jax.ShapeDtypeStruct(x.shape, x.dtype) for x in arrays],
        in_specs=[pl.BlockSpec(memory_space=pl.ANY)] * (len(arrays) + len(after)),
        out_specs=[pl.BlockSpec(memory_space=pl.ANY)] * len(arrays),
        input_output_aliases={n: n for n in range(len(arrays))},
        cost_estimate=pl.CostEstimate(flops=0, transcendentals=0, bytes_accessed=0),
        name="hold",
    )(*arrays, *after)


def turn(tiles, odd1, odd2):
    tiles = list(tiles)
    for bit, odd in ((1, odd1), (2, odd2)):
        for n in range(SPOTS):
            if n & bit == 0:
                a, b = tiles[n], tiles[n + bit]
                tiles[n] = jnp.where(odd, pltpu.roll(b, bit, a.ndim - 2), a)
                tiles[n + bit] = jnp.where(odd, b, pltpu.roll(a, SUB - bit, a.ndim - 2))
    return tiles


class Sizes:
    def __init__(self, both, deep):
        self.both, self.deep = both, deep
        self.own = SPOTS * deep
        self.cross = SPOTS * both * deep
        self.full = self.own + 3 * self.cross
        self.part = self.own + 2 * self.cross
        self.near = 2 * self.full
        self.far = 2 * self.part + self.cross
        self.own_rows = SPOTS * SPOTS
        self.cross_rows = SPOTS * SPOTS * both
        self.rows = PLANES * self.own_rows + 6 * self.cross_rows

    def cross_row(self, a, b):
        at = a * PLANES - a * (a + 1) // 2 + b - a - 1
        return PLANES * self.own_rows + self.cross_rows * at


def orient_kernel(sizes, where_ref, *refs):
    z, q = where_ref[0], where_ref[1]
    y_refs = refs[:SPOTS]
    kept, near, far, held = refs[-4:]
    both, deep, lanes = sizes.both, sizes.deep, y_refs[0].shape[-1]
    own, cross = sizes.own, sizes.cross
    spot = lax.broadcasted_iota(jnp.int32, (deep, SUB, lanes), 1)
    odd1, odd2 = (spot & 1) != 0, (spot & 2) != 0
    full = [0, own, own + cross, own + 2 * cross]
    places = {
        0: (kept, full),
        1: (near, [sizes.full + n for n in full]),
        2: (far, [0, 2 * sizes.part, own, own + cross]),
        3: (near, [0, sizes.part, own, own + cross]),
    }
    for dr in range(PLANES):
        out, firsts = places[dr]
        for br in range(PLANES):
            first = firsts[br]
            for m, y_ref in enumerate(y_refs):
                held[q ^ m] = y_ref[dr, br]

            def turned(u):
                return turn([held[n, u] for n in range(SPOTS)], odd1, odd2)

            if br == 0:
                other = turned(both - 1)
                for n in range(SPOTS):
                    out[first + n * deep : first + (n + 1) * deep] = held[n, 0] + other[n]
            else:
                lower = (z & (1 if br == 1 else 2)) == 0

                @pl.when(lower)
                def _():
                    for n in range(SPOTS):
                        for u in range(both):
                            at = first + (n * both + u) * deep
                            out[at : at + deep] = held[n, u]

                @pl.when(jnp.logical_not(lower))
                def _():
                    for u in range(both):
                        tiles = turned(both - 1 - u)
                        for n in range(SPOTS):
                            at = first + (n * both + u) * deep
                            out[at : at + deep] = tiles[n]


def orient(where, ys, sizes, after):
    lanes = ys[0].shape[-1]
    counts = (sizes.full, sizes.near, sizes.far)

    def kernel(*refs):
        orient_kernel(sizes, *refs)

    return pl.pallas_call(
        kernel,
        out_shape=[jax.ShapeDtypeStruct((n, SUB, lanes), jnp.float32) for n in counts],
        grid_spec=pltpu.PrefetchScalarGridSpec(
            num_scalar_prefetch=1,
            grid=(lanes // 128,),
            in_specs=[pl.BlockSpec(ys[0].shape[:-1] + (128,), lambda l, w: (0, 0, 0, 0, 0, l))]
            * SPOTS
            + [pl.BlockSpec(memory_space=pl.ANY)] * len(after),
            out_specs=[pl.BlockSpec((n, SUB, 128), lambda l, w: (0, 0, l)) for n in counts],
            scratch_shapes=[pltpu.VMEM((SPOTS, sizes.both, sizes.deep, SUB, 128), jnp.float32)],
        ),
        compiler_params=pltpu.CompilerParams(vmem_limit_bytes=VMEM),
        cost_estimate=pl.CostEstimate(
            flops=0, transcendentals=0, bytes_accessed=0
        ),
        name="orient",
    )(where, *ys, *after)


def merge(far, arrived, sizes, after):
    own, lanes = sizes.own, far.shape[-1]
    relayed = sizes.part // own

    def kernel(far_ref, arrived_ref, *rest):
        out_ref, token_ref = rest[-2:]
        n = pl.program_id(0)

        @pl.when(n < relayed)
        def _():
            out_ref[...] = arrived_ref[...]

        @pl.when(n >= relayed)
        def _():
            out_ref[...] = arrived_ref[...] + far_ref[...]

        token_ref[...] = jnp.zeros_like(token_ref)

    return pl.pallas_call(
        kernel,
        out_shape=[
            jax.ShapeDtypeStruct(far.shape, jnp.float32),
            jax.ShapeDtypeStruct((SUB, 128), jnp.float32),
        ],
        grid=(sizes.full // own,),
        in_specs=[
            pl.BlockSpec((own, SUB, lanes), lambda n: (jnp.maximum(n, relayed) + relayed, 0, 0)),
            pl.BlockSpec((own, SUB, lanes), lambda n: (n, 0, 0)),
        ]
        + [pl.BlockSpec(memory_space=pl.ANY)] * len(after),
        out_specs=[
            pl.BlockSpec((own, SUB, lanes), lambda n: (n + relayed, 0, 0)),
            pl.BlockSpec((SUB, 128), lambda n: (0, 0)),
        ],
        input_output_aliases={0: 0},
        compiler_params=pltpu.CompilerParams(vmem_limit_bytes=VMEM),
        cost_estimate=pl.CostEstimate(
            flops=0, transcendentals=0, bytes_accessed=0
        ),
        name="merge",
    )(far, arrived, *after)


def place_of(z, sizes):
    def cross(m, n):
        a, b = z ^ m, z ^ n
        return sizes.cross_row(jnp.minimum(a, b), jnp.maximum(a, b))

    own = [(z ^ n) * sizes.own_rows for n in range(PLANES)]
    pairs = [cross(0, 1), cross(0, 2), cross(0, 3), cross(1, 3), cross(1, 2), cross(2, 3)]
    return jnp.stack(own + pairs + [lax.axis_index("vir")]).astype(jnp.int32)


def multiply_kernel(spans, place_ref, *refs):
    b_ref, mine, theirs, hi, lo = refs[3 * len(spans)], *refs[-4:]
    lanes = refs[0].shape[-1]

    def gather(sizes, begin, kept, near, far):
        deep, own, cross, part = sizes.deep, sizes.own, sizes.cross, sizes.part
        pieces = [
            (kept, 0, None, 0, 1),
            (near, 0, None, 0, 1),
            (far, 0, None, 0, 1),
            (far, part, None, 0, 1),
            (kept, own, near, own, sizes.both),
            (kept, own + cross, far, own, sizes.both),
            (kept, own + 2 * cross, far, part + own + cross, sizes.both),
            (near, own + cross, far, part + own, sizes.both),
            (near, own + 2 * cross, far, own + cross, sizes.both),
            (far, 2 * part, None, 0, sizes.both),
        ]
        low = lax.broadcasted_iota(jnp.int32, (SUB, lanes), 0) < 4

        def step(k, carry):
            for at, (one, first, two, second, groups) in enumerate(pieces):
                for n in range(groups):
                    t = []
                    for m in range(4 * n, 4 * n + 4):
                        tile = one[first + m * deep + k]
                        if two is not None:
                            tile = tile + two[second + m * deep + k]
                        t.append(tile)
                    row = pl.multiple_of(place_ref[at] + 16 * n, 16)
                    x0 = [jnp.where(low, t[m], pltpu.roll(t[m + 1], 4, 0)) for m in (0, 2)]
                    x1 = [jnp.where(low, pltpu.roll(t[m], 4, 0), t[m + 1]) for m in (0, 2)]
                    for cg, x in enumerate((x0, x1)):
                        x = jnp.concatenate(x, axis=0)
                        top = x.astype(jnp.bfloat16)
                        column = pl.multiple_of((2 * (begin + k) + cg) * lanes, 128)
                        hi[pl.ds(row, 16), pl.ds(column, lanes)] = top
                        lo[pl.ds(row, 16), pl.ds(column, lanes)] = (
                            x - top.astype(jnp.float32)
                        ).astype(jnp.bfloat16)
            return carry

        lax.fori_loop(0, deep, step, 0)

    @pl.when(pl.program_id(0) == 0)
    def _():
        for at, (sizes, begin) in enumerate(spans):
            gather(sizes, begin, *refs[3 * at : 3 * at + 3])

    b = b_ref[...].reshape(b_ref.shape[0] * b_ref.shape[1], b_ref.shape[2])
    b_hi = b.astype(jnp.bfloat16)
    b_lo = (b - b_hi.astype(jnp.float32)).astype(jnp.bfloat16)
    dot = lambda x, y: jnp.dot(x, y, preferred_element_type=jnp.float32)
    c = dot(lo[...], b_hi) + dot(hi[...], b_lo) + dot(hi[...], b_hi)
    half = pl.num_programs(0) // 2

    @pl.when(pl.program_id(0) < half)
    def _():
        theirs[...] = c

    @pl.when(pl.program_id(0) >= half)
    def _():
        mine[...] = c


def multiply(place, parts, integrals, after):
    cs, ds, columns = integrals.shape
    rows = parts[0][0].rows
    wide = 256
    half = columns // wide // 2
    arrays = [x for _, _, three in parts for x in three]
    lanes = arrays[0].shape[-1]
    in_specs = []
    for sizes, _, _ in parts:
        in_specs += [
            pl.BlockSpec((sizes.full, SUB, lanes), lambda n, w: (0, 0, 0)),
            pl.BlockSpec((sizes.full, SUB, lanes), lambda n, w: (1, 0, 0)),
            pl.BlockSpec((sizes.far, SUB, lanes), lambda n, w: (0, 0, 0)),
        ]

    def kernel(*refs):
        multiply_kernel([(sizes, begin) for sizes, begin, _ in parts], *refs)

    def column(n, w):
        return lax.rem(n + (1 - w[PLANES + 6]) * half, 2 * half)

    return pl.pallas_call(
        kernel,
        out_shape=[jax.ShapeDtypeStruct((rows, columns // 2), jnp.float32)] * 2,
        grid_spec=pltpu.PrefetchScalarGridSpec(
            num_scalar_prefetch=1,
            grid=(2 * half,),
            in_specs=in_specs
            + [pl.BlockSpec((cs, ds, wide), lambda n, w: (0, 0, column(n, w)))]
            + [pl.BlockSpec(memory_space=pl.ANY)] * len(after),
            out_specs=[
                pl.BlockSpec((rows, wide), lambda n, w: (0, jnp.maximum(n - half, 0))),
                pl.BlockSpec((rows, wide), lambda n, w: (0, jnp.minimum(n, half - 1))),
            ],
            scratch_shapes=[pltpu.VMEM((rows, cs * ds), jnp.bfloat16)] * 2,
        ),
        compiler_params=pltpu.CompilerParams(vmem_limit_bytes=VMEM),
        cost_estimate=pl.CostEstimate(
            flops=0,
            transcendentals=0,
            bytes_accessed=0
        ),
        name="multiply",
    )(place, *arrays, integrals, *after)


def row_table(sizes):
    table = []
    for owner in range(OWNERS):
        for u in range(sizes.both):
            for partner in range(OWNERS):
                (za, qa), (zb, qb) = divmod(owner, SPOTS), divmod(partner, SPOTS)
                if (za, u) > (zb, 0) if za == zb else za > zb:
                    za, qa, zb, qb, v = zb, qb, za, qa, sizes.both - 1 - u
                else:
                    v = u
                if za == zb:
                    table.append(za * sizes.own_rows + qa * SPOTS + qb)
                else:
                    table.append(sizes.cross_row(za, zb) + (qa * sizes.both + v) * SPOTS + qb)
    return np.array(table, np.int32)


def spread(where, batch, after):
    classes = [sizes for sizes, _, _ in batch]
    table = np.concatenate([row_table(sizes) for sizes in classes])
    columns = batch[0][1].shape[1]
    rows = OWNERS * sum(sizes.both for sizes in classes)

    def kernel(where_ref, table_ref, *refs):
        z, q = where_ref[0], where_ref[1]
        outs = refs[-SPOTS:]
        begin = put = 0
        for at, sizes in enumerate(classes):
            one, two = refs[2 * at], refs[2 * at + 1]
            count = OWNERS * sizes.both
            for m, out in enumerate(outs):

                def step(n, carry):
                    dr, k = n // (count // 8), n % (count // 8)
                    first = begin + ((z ^ dr) * SPOTS + (q ^ m)) * count + k * 8
                    found = [pl.ds(table_ref[first + j], 1) for j in range(8)]
                    out[dr, pl.ds(pl.multiple_of(put + k * 8, 8), 8), :] = jnp.concatenate(
                        [one[row, :] + two[row, :] for row in found], axis=0
                    )
                    return carry

                lax.fori_loop(0, PLANES * count // 8, step, 0)
            begin += OWNERS * count
            put += count

    halves = [x for _, one, two in batch for x in (one, two)]
    return pl.pallas_call(
        kernel,
        out_shape=[jax.ShapeDtypeStruct((PLANES, rows, columns), jnp.float32)] * SPOTS,
        grid_spec=pltpu.PrefetchScalarGridSpec(
            num_scalar_prefetch=2,
            grid=(1,),
            in_specs=[pl.BlockSpec(x.shape, lambda n, w, t: (0, 0)) for x in halves]
            + [pl.BlockSpec(memory_space=pl.ANY)] * len(after),
            out_specs=[pl.BlockSpec((PLANES, rows, columns), lambda n, w, t: (0, 0, 0))] * SPOTS,
        ),
        compiler_params=pltpu.CompilerParams(vmem_limit_bytes=VMEM),
        cost_estimate=pl.CostEstimate(
            flops=0,
            transcendentals=0,
            bytes_accessed=0
        ),
        name="spread",
    )(where, jnp.asarray(table), *halves, *after)


def collect(batches):
    columns = batches[0][1][0].shape[1]
    arrays = [x for _, parts in batches for x in parts]

    def kernel(*refs):
        out = refs[-1]
        for at, (pairs, _) in enumerate(batches):
            a, b, c, d = refs[PLANES * at : PLANES * (at + 1)]
            for n, (r, s) in enumerate(pairs):
                rows = pl.ds(n * OWNERS, OWNERS)
                total = (a[rows, :] + b[rows, :]) + (c[rows, :] + d[rows, :])
                out[pl.ds(r * O + s, OWNERS, stride=SHARE), :] = total

    return pl.pallas_call(
        kernel,
        out_shape=jax.ShapeDtypeStruct((SHARE * O, columns), jnp.float32),
        grid=(columns // 128,),
        in_specs=[pl.BlockSpec((x.shape[0], 128), lambda n: (0, n)) for x in arrays],
        out_specs=pl.BlockSpec((SHARE * O, 128), lambda n: (0, n)),
        name="collect",
    )(*arrays)


def exchange(x, bits):
    return lax.ppermute(x, "occ", [(n, n ^ bits) for n in range(OWNERS)])


def in_planes(amplitudes, integrals):
    here = lax.axis_index("occ")
    z, q = here // SPOTS, here % SPOTS
    where = jnp.stack([z, q]).astype(jnp.int32)
    deep = amplitudes.shape[1] // CHUNK
    chunks = []
    for pair in CLASSES:
        chunks += [(pair, (0, deep // 2), False), (pair, (deep // 2, deep), True)]
    kepts, nears, tokens, fars, products = [], [], [], [], []
    parts, batch, batches, ready = [], [], [], []

    def last(arrays, back=1):
        return arrays[-back:][:1] if len(arrays) >= back else []

    def packed(at):
        pair, span, _ = chunks[at]
        return pack(where, amplitudes, pair, span, last(kepts))

    def first_half(at):
        own, *others = coming
        if kepts:
            others = hold(others, last(tokens, 1) + last(kepts))
        ys = [own] + [exchange(x, m) for m, x in enumerate(others, 1)]
        upcoming = packed(at + 1) if at + 1 < len(chunks) else []
        kept, near, far = orient(where, ys, sizes_of(at), list(upcoming[:1]))
        kepts.append(kept)
        nears.append((exchange(near, SPOTS), far))
        return upcoming

    def sizes_of(at):
        (r, s), span, _ = chunks[at]
        return Sizes(1 if r == s else 2, span[1] - span[0])

    def second_half(at, after):
        nonlocal parts, batch, ready
        (r, s), span, ends = chunks[at]
        parts.append((sizes_of(at), span[0], (kepts[at], nears[at][0], fars[at])))
        if not ends:
            return
        mine, theirs = multiply(place_of(z, sizes_of(at)), parts, integrals, ready + after)
        products.append(mine)
        theirs = lax.ppermute(theirs, "vir", [(0, 1), (1, 0)])
        batch.append((sizes_of(at), mine, theirs, [(r, s)] if r == s else [(r, s), (s, r)]))
        parts = []
        if (r, s) not in BATCH_ENDS:
            return
        before = nears[-1][:1] if batches else kepts[-1:]
        rows = spread(where, [x[:3] for x in batch], list(before))
        rows = [rows[0]] + [exchange(rows[m], m) for m in range(1, SPOTS)]
        plane = [rows[0][dr] + rows[1][dr] + rows[2][dr] + rows[3][dr] for dr in range(PLANES)]
        ready = plane[:1]
        batches.append(([pair for x in batch for pair in x[3]], plane))
        batch = []

    def over_planes(plane):
        return plane[:1] + [exchange(plane[dr], dr * SPOTS) for dr in range(1, PLANES)]

    coming = packed(0)
    coming = first_half(0)
    count = len(chunks)
    for at in range(count):
        if at + 1 < count:
            coming = first_half(at + 1)
        if at >= 2:
            second_half(at - 2, kepts[-1:] + (tokens[-1:] if at + 1 == count else []))
        before = last(fars, 2 if at + 2 == count else 1)
        if at >= 4:
            before = before + last(kepts) + last(products)
        near, far = nears[at]
        far, token = merge(far, near, sizes_of(at), before)
        tokens.append(token)
        fars.append(exchange(far, 2 * SPOTS))
    second_half(count - 2, [])
    early = [pair for pairs, _ in batches for pair in pairs]
    plane = [jnp.concatenate([x[dr] for _, x in batches]) for dr in range(PLANES)]
    second_half(count - 1, plane)
    return collect([(pairs, over_planes(x)) for pairs, x in [(early, plane), batches[-1]]])


def regrouped(amplitudes, integrals):
    moved = lax.all_to_all(amplitudes, "occ", split_axis=2, concat_axis=0, tiled=True)
    pair_count = moved.shape[0]
    col_count = moved.shape[1] * moved.shape[2]
    grouped = moved.reshape(O, O, col_count)
    summed = (grouped + jnp.transpose(grouped, (1, 0, 2))).reshape(pair_count, col_count)
    product = jnp.dot(
        summed,
        integrals.reshape(col_count, integrals.shape[2]),
        precision=lax.Precision.HIGHEST,
        preferred_element_type=jnp.float32,
    )
    half = lax.psum_scatter(product, "vir", scatter_dimension=1, tiled=True)
    return lax.psum_scatter(half, "occ", scatter_dimension=0, tiled=True)


def solution(mesh):
    def on_device(amplitudes, integrals):
        rows, cs, ds = amplitudes.shape
        fits = (
            mesh.shape["occ"] == OWNERS
            and mesh.shape["vir"] == 2
            and rows * OWNERS == O * O
            and cs % (2 * CHUNK) == 0
            and ds == 128 * 3
            and O == OWNERS * SHARE
            and integrals.shape[2] % 512 == 0
        )
        return in_planes(amplitudes, integrals) if fits else regrouped(amplitudes, integrals)

    in_specs = (P("occ", "vir", None), P("vir", "occ", None))
    out_specs = P("occ", "vir")
    return jax.shard_map(
        on_device, mesh=mesh, in_specs=in_specs, out_specs=out_specs, check_vma=False
    )
```

```python
import numpy as np
import jax
import jax.numpy as jnp
from jax import lax
from jax.experimental import pallas as pl
from jax.experimental.pallas import tpu as pltpu
from jax.sharding import PartitionSpec as P

O = 48
PLANES = 4
SPOTS = 4
OWNERS = PLANES * SPOTS
SHARE = O // OWNERS
CG = 16
SUB = 8
CHUNK = 2 * CG
VMEM = 56 * 1024 * 1024

CLASSES = ((0, 0), (1, 1), (0, 1), (0, 2), (1, 2), (2, 2))
BATCH_ENDS = ((0, 1), (0, 2), (1, 2), (2, 2))


def pack_kernel(where_ref, *refs):
    z, q = where_ref[0], where_ref[1]
    a_refs, x_refs, turned = refs[:3], refs[-SPOTS - 1 : -1], refs[-1]
    rows, cs, _ = a_refs[0].shape
    lanes = 128 * len(a_refs)
    width = lanes // OWNERS
    flat = [a_ref.reshape(rows * cs, 128) for a_ref in a_refs]
    lane = lax.broadcasted_iota(jnp.int32, (SUB, lanes), 1)
    block = (lane * (65536 // width + 1)) >> 16
    low = lax.broadcasted_iota(jnp.int32, (SUB, lanes), 0) < 4

    def step(half, carry):
        for cg in range(2):
            first = half * SUB * cs + cg * CG
            t = [
                jnp.concatenate([ref[pl.ds(first + c, SUB, stride=cs), :] for ref in flat], axis=1)
                for c in range(CG)
            ]
            for bit in (8, 4, 2, 1):
                keep = (block & bit) == 0
                for c in range(CG):
                    if c & bit == 0:
                        a, b = t[c], t[c + bit]
                        t[c] = jnp.where(keep, a, pltpu.roll(b, bit * width, 1))
                        t[c + bit] = jnp.where(keep, pltpu.roll(a, lanes - bit * width, 1), b)
            for o in range(OWNERS):
                turned[cg, o] = t[o]
        for m, x_ref in enumerate(x_refs):
            for dr in range(PLANES):
                o = (z ^ dr) * SPOTS + (q ^ m)
                t0, t1 = turned[0, o], turned[1, o]
                x_ref[dr, z ^ (2 * half)] = jnp.where(low, t0, pltpu.roll(t1, 4, 0))
                x_ref[dr, z ^ (2 * half + 1)] = jnp.where(low, pltpu.roll(t0, 4, 0), t1)
        return carry

    lax.fori_loop(0, 2, step, 0)


def pack(where, amplitudes, pair, span, after):
    r, s = pair
    both = 1 if r == s else 2
    rows, cs, lanes = amplitudes.shape
    begin, deep = span[0], span[1] - span[0]
    view = amplitudes.reshape(SHARE, OWNERS, SHARE, cs, lanes)
    shape = (PLANES, PLANES, both, deep, SUB, lanes)
    block = pl.BlockSpec(
        (PLANES, PLANES, None, None, SUB, lanes), lambda u, k, w: (0, 0, u, k, 0, 0)
    )
    in_specs = [
        pl.BlockSpec(
            (None, OWNERS, None, CHUNK, 128),
            lambda u, k, w, at=at: (r + u * (s - r), 0, s + u * (r - s), begin + k, at),
        )
        for at in range(lanes // 128)
    ]
    operands = [view] * len(in_specs) + after
    in_specs += [pl.BlockSpec(memory_space=pl.ANY)] * len(after)
    return pl.pallas_call(
        pack_kernel,
        out_shape=[jax.ShapeDtypeStruct(shape, jnp.float32)] * SPOTS,
        grid_spec=pltpu.PrefetchScalarGridSpec(
            num_scalar_prefetch=1,
            grid=(both, deep),
            in_specs=in_specs,
            out_specs=[block] * SPOTS,
            scratch_shapes=[pltpu.VMEM((2, OWNERS, SUB, lanes), jnp.float32)],
        ),
        compiler_params=pltpu.CompilerParams(vmem_limit_bytes=VMEM),
        cost_estimate=pl.CostEstimate(
            flops=0, transcendentals=0, bytes_accessed=0
        ),
        name="pack",
    )(where, *operands)


def hold(arrays, after):
    def kernel(*refs):
        pass

    return pl.pallas_call(
        kernel,
        out_shape=[jax.ShapeDtypeStruct(x.shape, x.dtype) for x in arrays],
        in_specs=[pl.BlockSpec(memory_space=pl.ANY)] * (len(arrays) + len(after)),
        out_specs=[pl.BlockSpec(memory_space=pl.ANY)] * len(arrays),
        input_output_aliases={n: n for n in range(len(arrays))},
        cost_estimate=pl.CostEstimate(flops=0, transcendentals=0, bytes_accessed=0),
        name="hold",
    )(*arrays, *after)


def turn(tiles, odd1, odd2):
    tiles = list(tiles)
    for bit, odd in ((1, odd1), (2, odd2)):
        for n in range(SPOTS):
            if n & bit == 0:
                a, b = tiles[n], tiles[n + bit]
                tiles[n] = jnp.where(odd, pltpu.roll(b, bit, a.ndim - 2), a)
                tiles[n + bit] = jnp.where(odd, b, pltpu.roll(a, SUB - bit, a.ndim - 2))
    return tiles


class Sizes:
    def __init__(self, both, deep):
        self.both, self.deep = both, deep
        self.own = SPOTS * deep
        self.cross = SPOTS * both * deep
        self.full = self.own + 3 * self.cross
        self.part = self.own + 2 * self.cross
        self.near = 2 * self.full
        self.far = 2 * self.part + self.cross
        self.own_rows = SPOTS * SPOTS
        self.cross_rows = SPOTS * SPOTS * both
        self.rows = PLANES * self.own_rows + 6 * self.cross_rows

    def cross_row(self, a, b):
        at = a * PLANES - a * (a + 1) // 2 + b - a - 1
        return PLANES * self.own_rows + self.cross_rows * at


def orient_kernel(sizes, where_ref, *refs):
    z, q = where_ref[0], where_ref[1]
    y_refs = refs[:SPOTS]
    kept, near, far, held = refs[-4:]
    both, deep, lanes = sizes.both, sizes.deep, y_refs[0].shape[-1]
    own, cross = sizes.own, sizes.cross
    spot = lax.broadcasted_iota(jnp.int32, (deep, SUB, lanes), 1)
    odd1, odd2 = (spot & 1) != 0, (spot & 2) != 0
    full = [0, own, own + cross, own + 2 * cross]
    places = {
        0: (kept, full),
        1: (near, [sizes.full + n for n in full]),
        2: (far, [0, 2 * sizes.part, own, own + cross]),
        3: (near, [0, sizes.part, own, own + cross]),
    }
    for dr in range(PLANES):
        out, firsts = places[dr]
        for br in range(PLANES):
            first = firsts[br]
            for m, y_ref in enumerate(y_refs):
                held[q ^ m] = y_ref[dr, br]

            def turned(u):
                return turn([held[n, u] for n in range(SPOTS)], odd1, odd2)

            if br == 0:
                other = turned(both - 1)
                for n in range(SPOTS):
                    out[first + n * deep : first + (n + 1) * deep] = held[n, 0] + other[n]
            else:
                lower = (z & (1 if br == 1 else 2)) == 0

                @pl.when(lower)
                def _():
                    for n in range(SPOTS):
                        for u in range(both):
                            at = first + (n * both + u) * deep
                            out[at : at + deep] = held[n, u]

                @pl.when(jnp.logical_not(lower))
                def _():
                    for u in range(both):
                        tiles = turned(both - 1 - u)
                        for n in range(SPOTS):
                            at = first + (n * both + u) * deep
                            out[at : at + deep] = tiles[n]


def orient(where, ys, sizes, after):
    lanes = ys[0].shape[-1]
    counts = (sizes.full, sizes.near, sizes.far)

    def kernel(*refs):
        orient_kernel(sizes, *refs)

    return pl.pallas_call(
        kernel,
        out_shape=[jax.ShapeDtypeStruct((n, SUB, lanes), jnp.float32) for n in counts],
        grid_spec=pltpu.PrefetchScalarGridSpec(
            num_scalar_prefetch=1,
            grid=(lanes // 128,),
            in_specs=[pl.BlockSpec(ys[0].shape[:-1] + (128,), lambda l, w: (0, 0, 0, 0, 0, l))]
            * SPOTS
            + [pl.BlockSpec(memory_space=pl.ANY)] * len(after),
            out_specs=[pl.BlockSpec((n, SUB, 128), lambda l, w: (0, 0, l)) for n in counts],
            scratch_shapes=[pltpu.VMEM((SPOTS, sizes.both, sizes.deep, SUB, 128), jnp.float32)],
        ),
        compiler_params=pltpu.CompilerParams(vmem_limit_bytes=VMEM),
        cost_estimate=pl.CostEstimate(
            flops=0, transcendentals=0, bytes_accessed=0
        ),
        name="orient",
    )(where, *ys, *after)


def merge(far, arrived, sizes, after):
    own, lanes = sizes.own, far.shape[-1]
    relayed = sizes.part // own

    def kernel(far_ref, arrived_ref, *rest):
        out_ref, token_ref = rest[-2:]
        n = pl.program_id(0)

        @pl.when(n < relayed)
        def _():
            out_ref[...] = arrived_ref[...]

        @pl.when(n >= relayed)
        def _():
            out_ref[...] = arrived_ref[...] + far_ref[...]

        token_ref[...] = jnp.zeros_like(token_ref)

    return pl.pallas_call(
        kernel,
        out_shape=[
            jax.ShapeDtypeStruct(far.shape, jnp.float32),
            jax.ShapeDtypeStruct((SUB, 128), jnp.float32),
        ],
        grid=(sizes.full // own,),
        in_specs=[
            pl.BlockSpec((own, SUB, lanes), lambda n: (jnp.maximum(n, relayed) + relayed, 0, 0)),
            pl.BlockSpec((own, SUB, lanes), lambda n: (n, 0, 0)),
        ]
        + [pl.BlockSpec(memory_space=pl.ANY)] * len(after),
        out_specs=[
            pl.BlockSpec((own, SUB, lanes), lambda n: (n + relayed, 0, 0)),
            pl.BlockSpec((SUB, 128), lambda n: (0, 0)),
        ],
        input_output_aliases={0: 0},
        compiler_params=pltpu.CompilerParams(vmem_limit_bytes=VMEM),
        cost_estimate=pl.CostEstimate(
            flops=0, transcendentals=0, bytes_accessed=0
        ),
        name="merge",
    )(far, arrived, *after)


def place_of(z, sizes):
    def cross(m, n):
        a, b = z ^ m, z ^ n
        return sizes.cross_row(jnp.minimum(a, b), jnp.maximum(a, b))

    own = [(z ^ n) * sizes.own_rows for n in range(PLANES)]
    pairs = [cross(0, 1), cross(0, 2), cross(0, 3), cross(1, 3), cross(1, 2), cross(2, 3)]
    return jnp.stack(own + pairs + [lax.axis_index("vir")]).astype(jnp.int32)


def multiply_kernel(parts, add, place_ref, *refs):
    b_ref, mine_in, theirs_in = refs[3 * len(parts) : 3 * len(parts) + 3]
    mine, theirs, hi, lo = refs[-4:]
    lanes = refs[0].shape[-1]

    def gather(sizes, begin, kept, near, far):
        deep, own, cross, part = sizes.deep, sizes.own, sizes.cross, sizes.part
        pieces = [
            (kept, 0, None, 0, 1),
            (near, 0, None, 0, 1),
            (far, 0, None, 0, 1),
            (far, part, None, 0, 1),
            (kept, own, near, own, sizes.both),
            (kept, own + cross, far, own, sizes.both),
            (kept, own + 2 * cross, far, part + own + cross, sizes.both),
            (near, own + cross, far, part + own, sizes.both),
            (near, own + 2 * cross, far, own + cross, sizes.both),
            (far, 2 * part, None, 0, sizes.both),
        ]
        low = lax.broadcasted_iota(jnp.int32, (SUB, lanes), 0) < 4

        def step(k, carry):
            for at, (one, first, two, second, groups) in enumerate(pieces):
                for n in range(groups):
                    t = []
                    for m in range(4 * n, 4 * n + 4):
                        tile = one[first + m * deep + k]
                        if two is not None:
                            tile = tile + two[second + m * deep + k]
                        t.append(tile)
                    row = pl.multiple_of(place_ref[at] + 16 * n, 16)
                    x0 = [jnp.where(low, t[m], pltpu.roll(t[m + 1], 4, 0)) for m in (0, 2)]
                    x1 = [jnp.where(low, pltpu.roll(t[m], 4, 0), t[m + 1]) for m in (0, 2)]
                    for cg, x in enumerate((x0, x1)):
                        x = jnp.concatenate(x, axis=0)
                        top = x.astype(jnp.bfloat16)
                        column = pl.multiple_of((2 * (begin + k) + cg) * lanes, 128)
                        hi[pl.ds(row, 16), pl.ds(column, lanes)] = top
                        lo[pl.ds(row, 16), pl.ds(column, lanes)] = (
                            x - top.astype(jnp.float32)
                        ).astype(jnp.bfloat16)
            return carry

        lax.fori_loop(0, deep, step, 0)

    @pl.when(pl.program_id(0) == 0)
    def _():
        begin = 0
        for at, sizes in enumerate(parts):
            gather(sizes, begin, *refs[3 * at : 3 * at + 3])
            begin += sizes.deep

    b = b_ref[...].reshape(b_ref.shape[0] * b_ref.shape[1], b_ref.shape[2])
    b_hi = b.astype(jnp.bfloat16)
    b_lo = (b - b_hi.astype(jnp.float32)).astype(jnp.bfloat16)
    dot = lambda x, y: jnp.dot(x, y, preferred_element_type=jnp.float32)
    c = dot(lo[...], b_hi) + dot(hi[...], b_lo) + dot(hi[...], b_hi)
    half = pl.num_programs(0) // 2

    @pl.when(pl.program_id(0) < half)
    def _():
        theirs[...] = c + theirs_in[...] if add else c

    @pl.when(pl.program_id(0) >= half)
    def _():
        mine[...] = c + mine_in[...] if add else c


def multiply(place, begin, parts, integrals, earlier, after):
    cs, ds, columns = integrals.shape
    lanes = parts[0][1][0].shape[-1]
    rows, deep = parts[0][0].rows, sum(sizes.deep for sizes, _ in parts)
    depth = deep * CHUNK
    wide = 256
    half = columns // wide // 2

    def kernel(*refs):
        multiply_kernel([sizes for sizes, _ in parts], len(earlier) > 0, *refs)

    def column(n, w):
        return lax.rem(n + (1 - w[PLANES + 6]) * half, 2 * half)

    out_specs = [
        pl.BlockSpec((rows, wide), lambda n, w: (0, jnp.maximum(n - half, 0))),
        pl.BlockSpec((rows, wide), lambda n, w: (0, jnp.minimum(n, half - 1))),
    ]
    in_specs = []
    for sizes, _ in parts:
        in_specs += [
            pl.BlockSpec((sizes.full, SUB, lanes), lambda n, w: (0, 0, 0)),
            pl.BlockSpec((sizes.full, SUB, lanes), lambda n, w: (1, 0, 0)),
            pl.BlockSpec((sizes.far, SUB, lanes), lambda n, w: (0, 0, 0)),
        ]
    in_specs.append(pl.BlockSpec((depth, ds, wide), lambda n, w: (begin // deep, 0, column(n, w))))
    return pl.pallas_call(
        kernel,
        out_shape=[jax.ShapeDtypeStruct((rows, columns // 2), jnp.float32)] * 2,
        grid_spec=pltpu.PrefetchScalarGridSpec(
            num_scalar_prefetch=1,
            grid=(2 * half,),
            in_specs=in_specs
            + out_specs[: len(earlier)]
            + [pl.BlockSpec(memory_space=pl.ANY)] * len(after),
            out_specs=out_specs,
            scratch_shapes=[pltpu.VMEM((rows, depth * ds), jnp.bfloat16)] * 2,
        ),
        compiler_params=pltpu.CompilerParams(vmem_limit_bytes=VMEM),
        cost_estimate=pl.CostEstimate(flops=0, transcendentals=0, bytes_accessed=0),
        name="multiply",
    )(place, *[x for _, arrays in parts for x in arrays], integrals, *earlier, *after)


def row_table(sizes):
    table = []
    for owner in range(OWNERS):
        for u in range(sizes.both):
            for partner in range(OWNERS):
                (za, qa), (zb, qb) = divmod(owner, SPOTS), divmod(partner, SPOTS)
                if (za, u) > (zb, 0) if za == zb else za > zb:
                    za, qa, zb, qb, v = zb, qb, za, qa, sizes.both - 1 - u
                else:
                    v = u
                if za == zb:
                    table.append(za * sizes.own_rows + qa * SPOTS + qb)
                else:
                    table.append(sizes.cross_row(za, zb) + (qa * sizes.both + v) * SPOTS + qb)
    return np.array(table, np.int32)


def spread(where, batch, after):
    classes = [sizes for sizes, _, _ in batch]
    table = np.concatenate([row_table(sizes) for sizes in classes])
    columns = batch[0][1].shape[1]
    rows = OWNERS * sum(sizes.both for sizes in classes)

    def kernel(where_ref, table_ref, *refs):
        z, q = where_ref[0], where_ref[1]
        outs = refs[-SPOTS:]
        begin = put = 0
        for at, sizes in enumerate(classes):
            one, two = refs[2 * at], refs[2 * at + 1]
            count = OWNERS * sizes.both
            for m, out in enumerate(outs):

                def step(n, carry):
                    dr, k = n // (count // 8), n % (count // 8)
                    first = begin + ((z ^ dr) * SPOTS + (q ^ m)) * count + k * 8
                    found = [pl.ds(table_ref[first + j], 1) for j in range(8)]
                    out[dr, pl.ds(pl.multiple_of(put + k * 8, 8), 8), :] = jnp.concatenate(
                        [one[row, :] + two[row, :] for row in found], axis=0
                    )
                    return carry

                lax.fori_loop(0, PLANES * count // 8, step, 0)
            begin += OWNERS * count
            put += count

    halves = [x for _, one, two in batch for x in (one, two)]
    return pl.pallas_call(
        kernel,
        out_shape=[jax.ShapeDtypeStruct((PLANES, rows, columns), jnp.float32)] * SPOTS,
        grid_spec=pltpu.PrefetchScalarGridSpec(
            num_scalar_prefetch=2,
            grid=(1,),
            in_specs=[pl.BlockSpec(x.shape, lambda n, w, t: (0, 0)) for x in halves]
            + [pl.BlockSpec(memory_space=pl.ANY)] * len(after),
            out_specs=[pl.BlockSpec((PLANES, rows, columns), lambda n, w, t: (0, 0, 0))] * SPOTS,
        ),
        compiler_params=pltpu.CompilerParams(vmem_limit_bytes=VMEM),
        cost_estimate=pl.CostEstimate(
            flops=0,
            transcendentals=0,
            bytes_accessed=0
        ),
        name="spread",
    )(where, jnp.asarray(table), *halves, *after)


def collect(batches):
    columns = batches[0][1][0].shape[1]
    arrays = [x for _, parts in batches for x in parts]

    def kernel(*refs):
        out = refs[-1]
        begin = 0
        for pairs, parts in batches:
            for n, (r, s) in enumerate(pairs):
                rows = pl.ds(n * OWNERS, OWNERS)
                total = refs[begin][rows, :]
                for at in range(1, len(parts)):
                    total = total + refs[begin + at][rows, :]
                out[pl.ds(r * O + s, OWNERS, stride=SHARE), :] = total
            begin += len(parts)

    return pl.pallas_call(
        kernel,
        out_shape=jax.ShapeDtypeStruct((SHARE * O, columns), jnp.float32),
        grid=(columns // 128,),
        in_specs=[pl.BlockSpec((x.shape[0], 128), lambda n: (0, n)) for x in arrays],
        out_specs=pl.BlockSpec((SHARE * O, 128), lambda n: (0, n)),
        name="collect",
    )(*arrays)


def exchange(x, bits):
    return lax.ppermute(x, "occ", [(n, n ^ bits) for n in range(OWNERS)])


def in_planes(amplitudes, integrals):
    here = lax.axis_index("occ")
    z, q = here // SPOTS, here % SPOTS
    where = jnp.stack([z, q]).astype(jnp.int32)
    deep = amplitudes.shape[1] // CHUNK
    chunks = []
    for pair in CLASSES:
        chunks += [(pair, (0, deep // 2), False), (pair, (deep // 2, deep), True)]
    kepts, nears, tokens, fars, products = [], [], [], [], []
    parts, earlier, batch, batches, ready = [], [], [], [], []

    def last(arrays, back=1):
        return arrays[-back:][:1] if len(arrays) >= back else []

    def packed(at):
        pair, span, _ = chunks[at]
        return pack(where, amplitudes, pair, span, last(kepts))

    def sizes_of(at):
        (r, s), span, _ = chunks[at]
        return Sizes(1 if r == s else 2, span[1] - span[0])

    def first_half(at):
        own, *others = coming
        if kepts:
            others = hold(others, last(tokens) + last(kepts))
        ys = [own] + [exchange(x, m) for m, x in enumerate(others, 1)]
        upcoming = packed(at + 1) if at + 1 < count else []
        kept, near, far = orient(where, ys, sizes_of(at), list(upcoming[:1]))
        kepts.append(kept)
        nears.append((exchange(near, SPOTS), far))
        return upcoming

    def second_half(at, after, until=[]):
        nonlocal earlier, parts, batch, ready
        (r, s), span, ends = chunks[at]
        sizes = sizes_of(at)
        parts.append((sizes, (kepts[at], nears[at][0], fars[at])))
        if not ends and (r, s) != CLASSES[-1]:
            return
        begin = span[1] - sum(part.deep for part, _ in parts)
        after = ready + after
        earlier = multiply(place_of(z, sizes), begin, parts, integrals, earlier, after)
        parts = []
        if not ends:
            return
        mine, theirs = earlier
        products.append(mine)
        earlier = []
        pairs = [(r, s)] if r == s else [(r, s), (s, r)]
        batch.append((sizes, mine, lax.ppermute(theirs, "vir", [(0, 1), (1, 0)]), pairs))
        if (r, s) not in BATCH_ENDS:
            return
        before = list(nears[-1][:1] if batches else kepts[-1:])
        rows = spread(where, [x[:3] for x in batch], before)
        rows = [rows[0]] + [exchange(rows[m], m) for m in range(1, SPOTS)]
        if until:
            rows = hold(rows, until)
        plane = [rows[0][n] + rows[1][n] + rows[2][n] + rows[3][n] for n in range(PLANES)]
        ready = plane[:1]
        batches.append(([pair for x in batch for pair in x[3]], plane))
        batch = []

    def over_planes(plane):
        return plane[:1] + [exchange(plane[dr], dr * SPOTS) for dr in range(1, PLANES)]

    count = len(chunks)
    coming = packed(0)
    coming = first_half(0)
    for at in range(count):
        if at + 1 < count:
            coming = first_half(at + 1)
        if at >= 2:
            after = tokens[-1:] if at + 1 == count else []
            second_half(at - 2, kepts[-1:] + after)
        before = last(fars, 2 if at + 2 == count else 1)
        if at >= 4:
            before = before + last(kepts) + last(products)
        near, far = nears[at]
        far, token = merge(far, near, sizes_of(at), before)
        tokens.append(token)
        fars.append(exchange(far, 2 * SPOTS))
    second_half(count - 2, [])
    early = [pair for pairs, _ in batches for pair in pairs]
    plane = [jnp.concatenate([x[n] for _, x in batches]) for n in range(PLANES)]
    sums = over_planes(plane)
    second_half(count - 1, plane, sums[1:])
    pairs, plane = batches[-1]
    return collect([(early, sums), (pairs, over_planes(plane))])


def regrouped(amplitudes, integrals):
    moved = lax.all_to_all(amplitudes, "occ", split_axis=2, concat_axis=0, tiled=True)
    pair_count = moved.shape[0]
    col_count = moved.shape[1] * moved.shape[2]
    grouped = moved.reshape(O, O, col_count)
    summed = (grouped + jnp.transpose(grouped, (1, 0, 2))).reshape(pair_count, col_count)
    product = jnp.dot(
        summed,
        integrals.reshape(col_count, integrals.shape[2]),
        precision=lax.Precision.HIGHEST,
        preferred_element_type=jnp.float32,
    )
    half = lax.psum_scatter(product, "vir", scatter_dimension=1, tiled=True)
    return lax.psum_scatter(half, "occ", scatter_dimension=0, tiled=True)


def solution(mesh):
    def on_device(amplitudes, integrals):
        rows, cs, ds = amplitudes.shape
        fits = (
            mesh.shape["occ"] == OWNERS
            and mesh.shape["vir"] == 2
            and rows * OWNERS == O * O
            and cs % (2 * CHUNK) == 0
            and ds == 128 * 3
            and O == OWNERS * SHARE
            and integrals.shape[2] % 512 == 0
        )
        return in_planes(amplitudes, integrals) if fits else regrouped(amplitudes, integrals)

    in_specs = (P("occ", "vir", None), P("vir", "occ", None))
    out_specs = P("occ", "vir")
    return jax.shard_map(
        on_device, mesh=mesh, in_specs=in_specs, out_specs=out_specs, check_vma=False
    )
```

```python
import numpy as np
import jax
import jax.numpy as jnp
from jax import lax
from jax.experimental import pallas as pl
from jax.experimental.pallas import tpu as pltpu
from jax.sharding import PartitionSpec as P

O = 48
PLANES = 4
SPOTS = 4
OWNERS = PLANES * SPOTS
SHARE = O // OWNERS
CG = 16
SUB = 8
CHUNK = 2 * CG
VMEM = 56 * 1024 * 1024

CLASSES = ((0, 0), (1, 1), (0, 1), (0, 2), (1, 2), (2, 2))
BATCH_ENDS = ((0, 1), (0, 2), (1, 2), (2, 2))


def pack_kernel(where_ref, *refs):
    z, q = where_ref[0], where_ref[1]
    a_refs, x_refs, turned = refs[:3], refs[-SPOTS - 1 : -1], refs[-1]
    rows, cs, _ = a_refs[0].shape
    lanes = 128 * len(a_refs)
    width = lanes // OWNERS
    flat = [a_ref.reshape(rows * cs, 128) for a_ref in a_refs]
    lane = lax.broadcasted_iota(jnp.int32, (SUB, lanes), 1)
    block = (lane * (65536 // width + 1)) >> 16
    low = lax.broadcasted_iota(jnp.int32, (SUB, lanes), 0) < 4

    def step(half, carry):
        for cg in range(2):
            first = half * SUB * cs + cg * CG
            t = [
                jnp.concatenate([ref[pl.ds(first + c, SUB, stride=cs), :] for ref in flat], axis=1)
                for c in range(CG)
            ]
            for bit in (8, 4, 2, 1):
                keep = (block & bit) == 0
                for c in range(CG):
                    if c & bit == 0:
                        a, b = t[c], t[c + bit]
                        t[c] = jnp.where(keep, a, pltpu.roll(b, bit * width, 1))
                        t[c + bit] = jnp.where(keep, pltpu.roll(a, lanes - bit * width, 1), b)
            for o in range(OWNERS):
                turned[cg, o] = t[o]
        for m, x_ref in enumerate(x_refs):
            for dr in range(PLANES):
                o = (z ^ dr) * SPOTS + (q ^ m)
                t0, t1 = turned[0, o], turned[1, o]
                x_ref[dr, z ^ (2 * half)] = jnp.where(low, t0, pltpu.roll(t1, 4, 0))
                x_ref[dr, z ^ (2 * half + 1)] = jnp.where(low, pltpu.roll(t0, 4, 0), t1)
        return carry

    lax.fori_loop(0, 2, step, 0)


def pack(where, amplitudes, pair, span, after):
    r, s = pair
    both = 1 if r == s else 2
    rows, cs, lanes = amplitudes.shape
    begin, deep = span[0], span[1] - span[0]
    view = amplitudes.reshape(SHARE, OWNERS, SHARE, cs, lanes)
    shape = (PLANES, PLANES, both, deep, SUB, lanes)
    block = pl.BlockSpec(
        (PLANES, PLANES, None, None, SUB, lanes), lambda u, k, w: (0, 0, u, k, 0, 0)
    )
    in_specs = [
        pl.BlockSpec(
            (None, OWNERS, None, CHUNK, 128),
            lambda u, k, w, at=at: (r + u * (s - r), 0, s + u * (r - s), begin + k, at),
        )
        for at in range(lanes // 128)
    ]
    operands = [view] * len(in_specs) + after
    in_specs += [pl.BlockSpec(memory_space=pl.ANY)] * len(after)
    return pl.pallas_call(
        pack_kernel,
        out_shape=[jax.ShapeDtypeStruct(shape, jnp.float32)] * SPOTS,
        grid_spec=pltpu.PrefetchScalarGridSpec(
            num_scalar_prefetch=1,
            grid=(both, deep),
            in_specs=in_specs,
            out_specs=[block] * SPOTS,
            scratch_shapes=[pltpu.VMEM((2, OWNERS, SUB, lanes), jnp.float32)],
        ),
        compiler_params=pltpu.CompilerParams(vmem_limit_bytes=VMEM),
        cost_estimate=pl.CostEstimate(
            flops=0, transcendentals=0, bytes_accessed=0
        ),
        name="pack",
    )(where, *operands)


def hold(arrays, after):
    def kernel(*refs):
        pass

    return pl.pallas_call(
        kernel,
        out_shape=[jax.ShapeDtypeStruct(x.shape, x.dtype) for x in arrays],
        in_specs=[pl.BlockSpec(memory_space=pl.ANY)] * (len(arrays) + len(after)),
        out_specs=[pl.BlockSpec(memory_space=pl.ANY)] * len(arrays),
        input_output_aliases={n: n for n in range(len(arrays))},
        cost_estimate=pl.CostEstimate(flops=0, transcendentals=0, bytes_accessed=0),
        name="hold",
    )(*arrays, *after)


def turn(tiles, odd1, odd2):
    tiles = list(tiles)
    for bit, odd in ((1, odd1), (2, odd2)):
        for n in range(SPOTS):
            if n & bit == 0:
                a, b = tiles[n], tiles[n + bit]
                tiles[n] = jnp.where(odd, pltpu.roll(b, bit, a.ndim - 2), a)
                tiles[n + bit] = jnp.where(odd, b, pltpu.roll(a, SUB - bit, a.ndim - 2))
    return tiles


class Sizes:
    def __init__(self, both, deep):
        self.both, self.deep = both, deep
        self.own = SPOTS * deep
        self.cross = SPOTS * both * deep
        self.full = self.own + 3 * self.cross
        self.part = self.own + 2 * self.cross
        self.near = 2 * self.full
        self.far = 2 * self.part + self.cross
        self.own_rows = SPOTS * SPOTS
        self.cross_rows = SPOTS * SPOTS * both
        self.rows = PLANES * self.own_rows + 6 * self.cross_rows

    def cross_row(self, a, b):
        at = a * PLANES - a * (a + 1) // 2 + b - a - 1
        return PLANES * self.own_rows + self.cross_rows * at


def orient_kernel(sizes, where_ref, *refs):
    z, q = where_ref[0], where_ref[1]
    y_refs = refs[:SPOTS]
    kept, near, far, held = refs[-4:]
    both, deep, lanes = sizes.both, sizes.deep, y_refs[0].shape[-1]
    own, cross = sizes.own, sizes.cross
    spot = lax.broadcasted_iota(jnp.int32, (deep, SUB, lanes), 1)
    odd1, odd2 = (spot & 1) != 0, (spot & 2) != 0
    full = [0, own, own + cross, own + 2 * cross]
    places = {
        0: (kept, full),
        1: (near, [sizes.full + n for n in full]),
        2: (far, [0, 2 * sizes.part, own, own + cross]),
        3: (near, [0, sizes.part, own, own + cross]),
    }
    for dr in range(PLANES):
        out, firsts = places[dr]
        for br in range(PLANES):
            first = firsts[br]
            for m, y_ref in enumerate(y_refs):
                held[q ^ m] = y_ref[dr, br]

            def turned(u):
                return turn([held[n, u] for n in range(SPOTS)], odd1, odd2)

            if br == 0:
                other = turned(both - 1)
                for n in range(SPOTS):
                    out[first + n * deep : first + (n + 1) * deep] = held[n, 0] + other[n]
            else:
                lower = (z & (1 if br == 1 else 2)) == 0

                @pl.when(lower)
                def _():
                    for n in range(SPOTS):
                        for u in range(both):
                            at = first + (n * both + u) * deep
                            out[at : at + deep] = held[n, u]

                @pl.when(jnp.logical_not(lower))
                def _():
                    for u in range(both):
                        tiles = turned(both - 1 - u)
                        for n in range(SPOTS):
                            at = first + (n * both + u) * deep
                            out[at : at + deep] = tiles[n]


def orient(where, ys, sizes, after):
    lanes = ys[0].shape[-1]
    counts = (sizes.full, sizes.near, sizes.far)

    def kernel(*refs):
        orient_kernel(sizes, *refs)

    return pl.pallas_call(
        kernel,
        out_shape=[jax.ShapeDtypeStruct((n, SUB, lanes), jnp.float32) for n in counts],
        grid_spec=pltpu.PrefetchScalarGridSpec(
            num_scalar_prefetch=1,
            grid=(lanes // 128,),
            in_specs=[pl.BlockSpec(ys[0].shape[:-1] + (128,), lambda l, w: (0, 0, 0, 0, 0, l))]
            * SPOTS
            + [pl.BlockSpec(memory_space=pl.ANY)] * len(after),
            out_specs=[pl.BlockSpec((n, SUB, 128), lambda l, w: (0, 0, l)) for n in counts],
            scratch_shapes=[pltpu.VMEM((SPOTS, sizes.both, sizes.deep, SUB, 128), jnp.float32)],
        ),
        compiler_params=pltpu.CompilerParams(vmem_limit_bytes=VMEM),
        cost_estimate=pl.CostEstimate(
            flops=0, transcendentals=0, bytes_accessed=0
        ),
        name="orient",
    )(where, *ys, *after)


def merge(far, arrived, sizes, after):
    own, lanes = sizes.own, far.shape[-1]
    relayed = sizes.part // own

    def kernel(far_ref, arrived_ref, *rest):
        out_ref, token_ref = rest[-2:]
        n = pl.program_id(0)

        @pl.when(n < relayed)
        def _():
            out_ref[...] = arrived_ref[...]

        @pl.when(n >= relayed)
        def _():
            out_ref[...] = arrived_ref[...] + far_ref[...]

        token_ref[...] = jnp.zeros_like(token_ref)

    return pl.pallas_call(
        kernel,
        out_shape=[
            jax.ShapeDtypeStruct(far.shape, jnp.float32),
            jax.ShapeDtypeStruct((SUB, 128), jnp.float32),
        ],
        grid=(sizes.full // own,),
        in_specs=[
            pl.BlockSpec((own, SUB, lanes), lambda n: (jnp.maximum(n, relayed) + relayed, 0, 0)),
            pl.BlockSpec((own, SUB, lanes), lambda n: (n, 0, 0)),
        ]
        + [pl.BlockSpec(memory_space=pl.ANY)] * len(after),
        out_specs=[
            pl.BlockSpec((own, SUB, lanes), lambda n: (n + relayed, 0, 0)),
            pl.BlockSpec((SUB, 128), lambda n: (0, 0)),
        ],
        input_output_aliases={0: 0},
        compiler_params=pltpu.CompilerParams(vmem_limit_bytes=VMEM),
        cost_estimate=pl.CostEstimate(
            flops=0, transcendentals=0, bytes_accessed=0
        ),
        name="merge",
    )(far, arrived, *after)


def place_of(z, sizes):
    def cross(m, n):
        a, b = z ^ m, z ^ n
        return sizes.cross_row(jnp.minimum(a, b), jnp.maximum(a, b))

    own = [(z ^ n) * sizes.own_rows for n in range(PLANES)]
    pairs = [cross(0, 1), cross(0, 2), cross(0, 3), cross(1, 3), cross(1, 2), cross(2, 3)]
    return jnp.stack(own + pairs + [lax.axis_index("vir")]).astype(jnp.int32)


def multiply_kernel(parts, add, place_ref, *refs):
    b_ref, mine_in, theirs_in = refs[3 * len(parts) : 3 * len(parts) + 3]
    mine, theirs, hi, lo = refs[-4:]
    lanes = refs[0].shape[-1]

    def gather(sizes, begin, kept, near, far):
        deep, own, cross, part = sizes.deep, sizes.own, sizes.cross, sizes.part
        pieces = [
            (kept, 0, None, 0, 1),
            (near, 0, None, 0, 1),
            (far, 0, None, 0, 1),
            (far, part, None, 0, 1),
            (kept, own, near, own, sizes.both),
            (kept, own + cross, far, own, sizes.both),
            (kept, own + 2 * cross, far, part + own + cross, sizes.both),
            (near, own + cross, far, part + own, sizes.both),
            (near, own + 2 * cross, far, own + cross, sizes.both),
            (far, 2 * part, None, 0, sizes.both),
        ]
        low = lax.broadcasted_iota(jnp.int32, (SUB, lanes), 0) < 4

        def step(k, carry):
            for at, (one, first, two, second, groups) in enumerate(pieces):
                for n in range(groups):
                    t = []
                    for m in range(4 * n, 4 * n + 4):
                        tile = one[first + m * deep + k]
                        if two is not None:
                            tile = tile + two[second + m * deep + k]
                        t.append(tile)
                    row = pl.multiple_of(place_ref[at] + 16 * n, 16)
                    x0 = [jnp.where(low, t[m], pltpu.roll(t[m + 1], 4, 0)) for m in (0, 2)]
                    x1 = [jnp.where(low, pltpu.roll(t[m], 4, 0), t[m + 1]) for m in (0, 2)]
                    for cg, x in enumerate((x0, x1)):
                        x = jnp.concatenate(x, axis=0)
                        top = x.astype(jnp.bfloat16)
                        column = pl.multiple_of((2 * (begin + k) + cg) * lanes, 128)
                        hi[pl.ds(row, 16), pl.ds(column, lanes)] = top
                        lo[pl.ds(row, 16), pl.ds(column, lanes)] = (
                            x - top.astype(jnp.float32)
                        ).astype(jnp.bfloat16)
            return carry

        lax.fori_loop(0, deep, step, 0)

    @pl.when(pl.program_id(0) == 0)
    def _():
        begin = 0
        for at, sizes in enumerate(parts):
            gather(sizes, begin, *refs[3 * at : 3 * at + 3])
            begin += sizes.deep

    b = b_ref[...].reshape(b_ref.shape[0] * b_ref.shape[1], b_ref.shape[2])
    b_hi = b.astype(jnp.bfloat16)
    b_lo = (b - b_hi.astype(jnp.float32)).astype(jnp.bfloat16)
    dot = lambda x, y: jnp.dot(x, y, preferred_element_type=jnp.float32)
    c = dot(lo[...], b_hi) + dot(hi[...], b_lo) + dot(hi[...], b_hi)
    half = pl.num_programs(0) // 2

    @pl.when(pl.program_id(0) < half)
    def _():
        theirs[...] = c + theirs_in[...] if add else c

    @pl.when(pl.program_id(0) >= half)
    def _():
        mine[...] = c + mine_in[...] if add else c


def multiply(place, begin, parts, integrals, earlier, after):
    cs, ds, columns = integrals.shape
    lanes = parts[0][1][0].shape[-1]
    rows, deep = parts[0][0].rows, sum(sizes.deep for sizes, _ in parts)
    depth = deep * CHUNK
    wide = 256
    half = columns // wide // 2

    def kernel(*refs):
        multiply_kernel([sizes for sizes, _ in parts], len(earlier) > 0, *refs)

    def column(n, w):
        return lax.rem(n + (1 - w[PLANES + 6]) * half, 2 * half)

    out_specs = [
        pl.BlockSpec((rows, wide), lambda n, w: (0, jnp.maximum(n - half, 0))),
        pl.BlockSpec((rows, wide), lambda n, w: (0, jnp.minimum(n, half - 1))),
    ]
    in_specs = []
    for sizes, _ in parts:
        in_specs += [
            pl.BlockSpec((sizes.full, SUB, lanes), lambda n, w: (0, 0, 0)),
            pl.BlockSpec((sizes.full, SUB, lanes), lambda n, w: (1, 0, 0)),
            pl.BlockSpec((sizes.far, SUB, lanes), lambda n, w: (0, 0, 0)),
        ]
    in_specs.append(pl.BlockSpec((depth, ds, wide), lambda n, w: (begin // deep, 0, column(n, w))))
    return pl.pallas_call(
        kernel,
        out_shape=[jax.ShapeDtypeStruct((rows, columns // 2), jnp.float32)] * 2,
        grid_spec=pltpu.PrefetchScalarGridSpec(
            num_scalar_prefetch=1,
            grid=(2 * half,),
            in_specs=in_specs
            + out_specs[: len(earlier)]
            + [pl.BlockSpec(memory_space=pl.ANY)] * len(after),
            out_specs=out_specs,
            scratch_shapes=[pltpu.VMEM((rows, depth * ds), jnp.bfloat16)] * 2,
        ),
        compiler_params=pltpu.CompilerParams(vmem_limit_bytes=VMEM),
        cost_estimate=pl.CostEstimate(flops=0, transcendentals=0, bytes_accessed=0),
        name="multiply",
    )(place, *[x for _, arrays in parts for x in arrays], integrals, *earlier, *after)


def row_table(sizes):
    table = []
    for owner in range(OWNERS):
        for u in range(sizes.both):
            for partner in range(OWNERS):
                (za, qa), (zb, qb) = divmod(owner, SPOTS), divmod(partner, SPOTS)
                if (za, u) > (zb, 0) if za == zb else za > zb:
                    za, qa, zb, qb, v = zb, qb, za, qa, sizes.both - 1 - u
                else:
                    v = u
                if za == zb:
                    table.append(za * sizes.own_rows + qa * SPOTS + qb)
                else:
                    table.append(sizes.cross_row(za, zb) + (qa * sizes.both + v) * SPOTS + qb)
    return np.array(table, np.int32)


def spread(where, batch, after):
    classes = [sizes for sizes, _, _ in batch]
    table = np.concatenate([row_table(sizes) for sizes in classes])
    columns = batch[0][1].shape[1]
    rows = OWNERS * sum(sizes.both for sizes in classes)

    def kernel(where_ref, table_ref, *refs):
        z, q = where_ref[0], where_ref[1]
        outs = refs[-SPOTS:]
        begin = put = 0
        for at, sizes in enumerate(classes):
            one, two = refs[2 * at], refs[2 * at + 1]
            count = OWNERS * sizes.both
            for m, out in enumerate(outs):

                def step(n, carry):
                    dr, k = n // (count // 8), n % (count // 8)
                    first = begin + ((z ^ dr) * SPOTS + (q ^ m)) * count + k * 8
                    found = [pl.ds(table_ref[first + j], 1) for j in range(8)]
                    out[dr, pl.ds(pl.multiple_of(put + k * 8, 8), 8), :] = jnp.concatenate(
                        [one[row, :] + two[row, :] for row in found], axis=0
                    )
                    return carry

                lax.fori_loop(0, PLANES * count // 8, step, 0)
            begin += OWNERS * count
            put += count

    halves = [x for _, one, two in batch for x in (one, two)]
    return pl.pallas_call(
        kernel,
        out_shape=[jax.ShapeDtypeStruct((PLANES, rows, columns), jnp.float32)] * SPOTS,
        grid_spec=pltpu.PrefetchScalarGridSpec(
            num_scalar_prefetch=2,
            grid=(1,),
            in_specs=[pl.BlockSpec(x.shape, lambda n, w, t: (0, 0)) for x in halves]
            + [pl.BlockSpec(memory_space=pl.ANY)] * len(after),
            out_specs=[pl.BlockSpec((PLANES, rows, columns), lambda n, w, t: (0, 0, 0))] * SPOTS,
        ),
        compiler_params=pltpu.CompilerParams(vmem_limit_bytes=VMEM),
        cost_estimate=pl.CostEstimate(
            flops=0,
            transcendentals=0,
            bytes_accessed=0
        ),
        name="spread",
    )(where, jnp.asarray(table), *halves, *after)


def collect(batches):
    columns = batches[0][1][0].shape[1]
    arrays = [x for _, parts in batches for x in parts]

    def kernel(*refs):
        out = refs[-1]
        begin = 0
        for pairs, parts in batches:
            for n, (r, s) in enumerate(pairs):
                rows = pl.ds(n * OWNERS, OWNERS)
                total = refs[begin][rows, :]
                for at in range(1, len(parts)):
                    total = total + refs[begin + at][rows, :]
                out[pl.ds(r * O + s, OWNERS, stride=SHARE), :] = total
            begin += len(parts)

    return pl.pallas_call(
        kernel,
        out_shape=jax.ShapeDtypeStruct((SHARE * O, columns), jnp.float32),
        grid=(columns // 128,),
        in_specs=[pl.BlockSpec((x.shape[0], 128), lambda n: (0, n)) for x in arrays],
        out_specs=pl.BlockSpec((SHARE * O, 128), lambda n: (0, n)),
        name="collect",
    )(*arrays)


def exchange(x, bits):
    return lax.ppermute(x, "occ", [(n, n ^ bits) for n in range(OWNERS)])


def in_planes(amplitudes, integrals):
    here = lax.axis_index("occ")
    z, q = here // SPOTS, here % SPOTS
    where = jnp.stack([z, q]).astype(jnp.int32)
    deep = amplitudes.shape[1] // CHUNK
    chunks = []
    for pair in CLASSES:
        chunks += [(pair, (0, deep // 2), False), (pair, (deep // 2, deep), True)]
    kepts, nears, tokens, fars, products = [], [], [], [], []
    parts, earlier, batch, batches, ready = [], [], [], [], []

    def last(arrays, back=1):
        return arrays[-back:][:1] if len(arrays) >= back else []

    def packed(at):
        pair, span, _ = chunks[at]
        return pack(where, amplitudes, pair, span, last(kepts))

    def sizes_of(at):
        (r, s), span, _ = chunks[at]
        return Sizes(1 if r == s else 2, span[1] - span[0])

    def first_half(at):
        own, *others = coming
        if kepts:
            others = hold(others, last(tokens, 2 if at in (3, 4) else 1) + last(kepts))
        ys = [own] + [exchange(x, m) for m, x in enumerate(others, 1)]
        upcoming = packed(at + 1) if at + 1 < count else []
        kept, near, far = orient(where, ys, sizes_of(at), list(upcoming[:1]))
        kepts.append(kept)
        nears.append((exchange(near, SPOTS), far))
        return upcoming

    def second_half(at, after, until=[]):
        nonlocal earlier, parts, batch, ready
        (r, s), span, ends = chunks[at]
        sizes = sizes_of(at)
        parts.append((sizes, (kepts[at], nears[at][0], fars[at])))
        if not ends and (r, s) not in CLASSES[-2:]:
            return
        begin = span[1] - sum(part.deep for part, _ in parts)
        after = ready + after
        earlier = multiply(place_of(z, sizes), begin, parts, integrals, earlier, after)
        parts = []
        if not ends:
            return
        mine, theirs = earlier
        products.append(mine)
        earlier = []
        pairs = [(r, s)] if r == s else [(r, s), (s, r)]
        batch.append((sizes, mine, lax.ppermute(theirs, "vir", [(0, 1), (1, 0)]), pairs))
        if (r, s) not in BATCH_ENDS:
            return
        before = list(nears[-1][:1] if batches else kepts[-1:])
        rows = spread(where, [x[:3] for x in batch], before)
        rows = [rows[0]] + [exchange(rows[m], m) for m in range(1, SPOTS)]
        if until:
            rows = hold(rows, until)
        plane = [rows[0][n] + rows[1][n] + rows[2][n] + rows[3][n] for n in range(PLANES)]
        ready = plane[:1]
        batches.append(([pair for x in batch for pair in x[3]], plane))
        batch = []

    def over_planes(plane):
        return plane[:1] + [exchange(plane[dr], dr * SPOTS) for dr in range(1, PLANES)]

    count = len(chunks)
    coming = packed(0)
    coming = first_half(0)
    for at in range(count):
        if at + 1 < count:
            coming = first_half(at + 1)
        if at >= 2:
            after = tokens[-1:] if at + 1 == count else []
            second_half(at - 2, kepts[-1:] + after)
        before = last(fars, 2 if at + 2 == count else 1)
        if at >= 4:
            before = before + last(kepts) + last(products)
        near, far = nears[at]
        far, token = merge(far, near, sizes_of(at), before)
        tokens.append(token)
        fars.append(exchange(far, 2 * SPOTS))
    second_half(count - 2, [])
    early = [pair for pairs, _ in batches for pair in pairs]
    plane = [jnp.concatenate([x[n] for _, x in batches]) for n in range(PLANES)]
    sums = over_planes(plane)
    second_half(count - 1, plane, sums[1:])
    pairs, plane = batches[-1]
    return collect([(early, sums), (pairs, over_planes(plane))])


def regrouped(amplitudes, integrals):
    moved = lax.all_to_all(amplitudes, "occ", split_axis=2, concat_axis=0, tiled=True)
    pair_count = moved.shape[0]
    col_count = moved.shape[1] * moved.shape[2]
    grouped = moved.reshape(O, O, col_count)
    summed = (grouped + jnp.transpose(grouped, (1, 0, 2))).reshape(pair_count, col_count)
    product = jnp.dot(
        summed,
        integrals.reshape(col_count, integrals.shape[2]),
        precision=lax.Precision.HIGHEST,
        preferred_element_type=jnp.float32,
    )
    half = lax.psum_scatter(product, "vir", scatter_dimension=1, tiled=True)
    return lax.psum_scatter(half, "occ", scatter_dimension=0, tiled=True)


def solution(mesh):
    def on_device(amplitudes, integrals):
        rows, cs, ds = amplitudes.shape
        fits = (
            mesh.shape["occ"] == OWNERS
            and mesh.shape["vir"] == 2
            and rows * OWNERS == O * O
            and cs % (2 * CHUNK) == 0
            and ds == 128 * 3
            and O == OWNERS * SHARE
            and integrals.shape[2] % 512 == 0
        )
        return in_planes(amplitudes, integrals) if fits else regrouped(amplitudes, integrals)

    in_specs = (P("occ", "vir", None), P("vir", "occ", None))
    out_specs = P("occ", "vir")
    return jax.shard_map(
        on_device, mesh=mesh, in_specs=in_specs, out_specs=out_specs, check_vma=False
    )
```
